512 devices in a mesh: rep: 16 (over z_lo, x, core), tp: 32 (over y, z_hi).
Axes of the slice: x: 4, y: 8, z: 8 (z_hi: 4, z_lo: 2; z = z_hi * 2 + z_lo), core: 2. Of those that a mesh axis runs over, the one named last changes fastest.
Arguments:
- queries: bfloat16 [65536, 4096], P(('rep', 'tp')), may hold values from -4.5 to 4.5
- keys: bfloat16 [65536, 512], P(('rep', 'tp')), may hold values from -4.5 to 4.5
- values: bfloat16 [65536, 512], P(('rep', 'tp')), may hold values from -6 to 6
- out_grad: bfloat16 [65536, 4096], P(('rep', 'tp')), may hold values from -6 to 6
- deltas: bfloat16 [8192, 8192], P('rep', 'tp'), may hold values from -6 to 6
- block_ids: int32 [1], replicated, may hold values from 0 to 1
- params: float32 [256, 8192], P(None, 'tp'), may hold values from -6 to 6
- momentum: float32 [256, 8192], P(None, 'tp'), may hold values from -3 to 3
Outputs:
- query_grad: bfloat16 [65536, 4096], P(('rep', 'tp'))
- key_gradient: bfloat16 [65536, 512], P(('rep', 'tp'))
- value_gradient: bfloat16 [65536, 512], P(('rep', 'tp'))
- params_out: float32 [256, 8192], P(None, 'tp')
- momentum_out: float32 [256, 8192], P(None, 'tp')
The draws below stay inside these ranges and needn't reach their ends.
All inputs are finite; a program needn't handle non-finite values.
Results may differ from the reference program's by a relative error of at most 0.0095.
Values may be sent and summed in bfloat16 or wider, within the bound.
No kernel may reach another device: no remote copies, remote signals or barrier semaphores. Data moves between devices by JAX's collectives and lax.ppermute only.
A program may use at most 128 MiB of HBM per device.

```python
import math
import jax
import jax.numpy as jnp
from jax import lax

D = 8192
QUERY_HEADS = 32
KEY_VALUE_HEADS = 4
HEAD_SIZE = 128
SEQUENCE_LENGTH = 2048
SEQS = 2
BLOCK = 256
FRAG = 2
LISTED = 1
ALL_POSITIONS = 65536
DELTA_ROWS = 8192
N_REP = 16


def draw_queries(key, part):
    key = jax.random.fold_in(key, 11)
    final_result = jax.random.truncated_normal(key, -4.5, 4.5, (ALL_POSITIONS, QUERY_HEADS * HEAD_SIZE), jnp.float32)
    return final_result.astype(jnp.bfloat16)


def draw_keys(key, part):
    key = jax.random.fold_in(key, 23)
    final_result = jax.random.truncated_normal(key, -4.5, 4.5, (ALL_POSITIONS, KEY_VALUE_HEADS * HEAD_SIZE), jnp.float32)
    return final_result.astype(jnp.bfloat16)


def shard_levels(stream_key, dims, shards, smallest, top_value):
    gain = 1.0
    for dim, shards_of in shards:
        heights = jax.random.uniform(jax.random.fold_in(jax.random.fold_in(stream_key, 6), dim), (shards_of,), jnp.float32, smallest / len(shards), top_value / len(shards))
        gain = gain * jnp.repeat(jnp.exp(heights), dims[dim] // shards_of).reshape((-1,) + (1,) * (len(dims) - 1 - dim))
    return gain


def scatter_about(own_key, shape, spread, most, shards=(), held_as=jnp.bfloat16):
    factor_of = shard_levels(own_key, shape, shards, -0.22, 0.18) if shards else 1.0
    result = jax.random.normal(own_key, shape, jnp.float32) * spread * factor_of
    return jnp.minimum(jnp.maximum(result, -most), most).astype(held_as)


def setup_inputs(seed: int = 0) -> dict:
    splits = jax.random.split(jax.random.key(seed), 9)
    queries = draw_queries(jax.random.fold_in(splits[8], 71), 0)
    keys = draw_keys(jax.random.fold_in(splits[8], 71), 0)
    values = scatter_about(splits[2], (ALL_POSITIONS, KEY_VALUE_HEADS * HEAD_SIZE), 1.0, 6.0, ((0, 512),))
    out_grad = scatter_about(splits[3], (ALL_POSITIONS, QUERY_HEADS * HEAD_SIZE), 1.0, 6.0, ((0, 512),))
    deltas = scatter_about(splits[4], (DELTA_ROWS, D), 1.0, 6.0, ((0, 16), (1, 32)))
    block_ids = jax.random.randint(splits[5], (LISTED,), 0, FRAG).astype(jnp.int32)
    params = scatter_about(splits[6], (LISTED * BLOCK, D), 1.0, 6.0, ((1, 32),), jnp.float32)
    momentum = scatter_about(splits[7], (LISTED * BLOCK, D), 0.5, 3.0, ((1, 32),), jnp.float32)
    return dict(queries=queries, keys=keys, values=values, out_grad=out_grad, deltas=deltas, block_ids=block_ids, params=params, momentum=momentum)


NEG_FILL = -1e+30
OUTER_LR = 0.7
OUTER_MU = 0.9

def head_grads(query_head, key_head, value_head, grad_head):
    head_width = query_head.shape[1]
    score_scale = 1.0 / math.sqrt(head_width)
    scores = jnp.dot(query_head, key_head.T, preferred_element_type=jnp.float32) * score_scale
    row_pos = lax.broadcasted_iota(jnp.int32, scores.shape, 0)
    col_pos = lax.broadcasted_iota(jnp.int32, scores.shape, 1)
    scores = jnp.where(row_pos >= col_pos, scores, NEG_FILL)
    row_peak = lax.optimization_barrier(jnp.max(scores, axis=1, keepdims=True))
    weights_raw = jnp.exp(scores - row_peak)
    prob_full = weights_raw / lax.optimization_barrier(jnp.sum(weights_raw, axis=1, keepdims=True))
    prob_low = prob_full.astype(jnp.bfloat16)
    prob_grad = jnp.dot(grad_head, value_head.T, preferred_element_type=jnp.float32)
    row_inner = lax.optimization_barrier(jnp.sum(prob_full * prob_grad, axis=1, keepdims=True))
    score_grad = (prob_full * (prob_grad - row_inner) * score_scale).astype(jnp.bfloat16)
    query_grad = jnp.dot(score_grad, key_head, preferred_element_type=jnp.float32)
    key_gradient = jnp.dot(score_grad.T, query_head, preferred_element_type=jnp.float32)
    value_gradient = jnp.dot(prob_low.T, grad_head, preferred_element_type=jnp.float32)
    return (query_grad, key_gradient, value_gradient)

def separate_heads(array, count):
    return array.reshape(N_REP * SEQS, SEQUENCE_LENGTH, count, HEAD_SIZE).transpose(0, 2, 1, 3)

def join_heads(array, count):
    return array.reshape(N_REP * SEQS, count, SEQUENCE_LENGTH, HEAD_SIZE).transpose(0, 2, 1, 3).reshape(N_REP * SEQS * SEQUENCE_LENGTH, count * HEAD_SIZE)

def reference(queries, keys, values, out_grad, deltas, block_ids, params, momentum):
    query_group = QUERY_HEADS // KEY_VALUE_HEADS
    sequence_count = N_REP * SEQS
    query_heads = separate_heads(queries, QUERY_HEADS).reshape(sequence_count * QUERY_HEADS, SEQUENCE_LENGTH, HEAD_SIZE)
    grad_heads = separate_heads(out_grad, QUERY_HEADS).reshape(sequence_count * QUERY_HEADS, SEQUENCE_LENGTH, HEAD_SIZE)
    key_head_rows = jnp.repeat(separate_heads(keys, KEY_VALUE_HEADS), query_group, axis=1).reshape(sequence_count * QUERY_HEADS, SEQUENCE_LENGTH, HEAD_SIZE)
    value_head_rows = jnp.repeat(separate_heads(values, KEY_VALUE_HEADS), query_group, axis=1).reshape(sequence_count * QUERY_HEADS, SEQUENCE_LENGTH, HEAD_SIZE)
    query_grad, key_gradient, value_gradient = lax.map(lambda items: head_grads(items[0], items[1], items[2], items[3]), (query_heads, key_head_rows, value_head_rows, grad_heads))
    query_out = join_heads(query_grad.astype(jnp.bfloat16), QUERY_HEADS)
    key_result = join_heads(key_gradient.reshape(sequence_count, KEY_VALUE_HEADS, query_group, SEQUENCE_LENGTH, HEAD_SIZE).sum(axis=2).astype(jnp.bfloat16), KEY_VALUE_HEADS)
    value_result = join_heads(value_gradient.reshape(sequence_count, KEY_VALUE_HEADS, query_group, SEQUENCE_LENGTH, HEAD_SIZE).sum(axis=2).astype(jnp.bfloat16), KEY_VALUE_HEADS)
    picked = deltas.reshape(N_REP, FRAG, BLOCK, D)[:, block_ids].astype(jnp.float32)
    outer_grad = lax.optimization_barrier(jnp.sum(picked, axis=0)).reshape(LISTED * BLOCK, D) / N_REP
    momentum_out = OUTER_MU * momentum + outer_grad
    params_out = params - OUTER_LR * (outer_grad + OUTER_MU * momentum_out)
    return (query_out, key_result, value_result, params_out, momentum_out)
```

```python
import functools
import math

import jax
import jax.numpy as jnp
from jax import lax
from jax.experimental import pallas as pl
from jax.experimental.pallas import tpu as pltpu
from jax.sharding import PartitionSpec as P

QUERY_HEADS = 32
KEY_VALUE_HEADS = 4
HEAD_SIZE = 128
SEQUENCE_LENGTH = 2048
SEQS = 2
BLOCK = 256
ROWS = 128
GROUP = QUERY_HEADS // KEY_VALUE_HEADS
NEG_FILL = -1e30
OUTER_LR = 0.7
OUTER_MU = 0.9
SCALE = HEAD_SIZE**-0.5
EXP2_SCALE = SCALE * math.log2(math.e)
LOW = jnp.bfloat16


def dot(a, b, dim_a, dim_b):
    return lax.dot_general(
        a, b, (((dim_a,), (dim_b,)), ((), ())), preferred_element_type=jnp.float32
    )


def attention_kernel(place, *refs):
    rows_in, keys_in = refs[:4], refs[4:8]
    dq_ref, dkv_refs = refs[8], refs[9:13]
    qs, gs, ks, vs, kt, dks, dvs = refs[13:]
    y, z = place[0], place[1]
    for slot in range(4):
        qs[slot] = rows_in[slot][0]
        gs[slot] = rows_in[slot][1]
        for j in range(4):
            ks[slot, j * ROWS : (j + 1) * ROWS] = keys_in[j][slot, 0]
            vs[slot, j * ROWS : (j + 1) * ROWS] = keys_in[j][slot, 1]
    for slot in range(4):
        kt[slot] = ks[slot].T
    width = 2 * HEAD_SIZE
    key_at = lax.broadcasted_iota(jnp.int32, (4 * ROWS, width), 0)
    row_at = lax.broadcasted_iota(jnp.int32, (4 * ROWS, width), 1) & (ROWS - 1)
    key_pos = (((key_at >> 7) ^ z) << 7) + (key_at & (ROWS - 1))
    keep = key_pos <= row_at + (z << 7)

    for group in range(3, -1, -1):
        row_slot = group ^ y

        def step(pair, carry, group=group, row_slot=row_slot):
            first = pl.multiple_of(pair * width, width)
            q_pair = qs[row_slot, :, pl.ds(first, width)]
            g_pair = gs[row_slot, :, pl.ds(first, width)]
            q = jnp.concatenate([q_pair[:, :HEAD_SIZE], q_pair[:, HEAD_SIZE:]], 0)
            g = jnp.concatenate([g_pair[:, :HEAD_SIZE], g_pair[:, HEAD_SIZE:]], 0)
            scores = []
            peak = None
            for part in range(group + 1):
                s = dot(ks[part ^ y], q, 1, 1)
                if part == group:
                    s = jnp.where(keep, s, NEG_FILL)
                scores.append(s)
                top = jnp.max(s, axis=0, keepdims=True)
                peak = top if peak is None else jnp.maximum(peak, top)
            shift = peak * EXP2_SCALE
            weights, prob_grads = [], []
            total = inner = None
            for part in range(group + 1):
                prob_grad = dot(vs[part ^ y], g, 1, 1)
                weight = jnp.exp2(scores[part] * EXP2_SCALE - shift)
                total_part = jnp.sum(weight, axis=0, keepdims=True)
                inner_part = jnp.sum(weight * prob_grad, axis=0, keepdims=True)
                total = total_part if total is None else total + total_part
                inner = inner_part if inner is None else inner + inner_part
                weights.append(weight)
                prob_grads.append(prob_grad)
            inverse = 1.0 / total
            inner = inner * inverse
            dq_t = None
            for part in range(group + 1):
                slot = part ^ y
                prob = weights[part] * inverse
                prob_low = prob.astype(LOW)
                score_grad = (prob * (prob_grads[part] - inner)).astype(LOW)
                dv = dot(prob_low, g, 1, 0)
                dk = dot(score_grad, q, 1, 0)
                if group == 3:

                    @pl.when(pair == 0)
                    def _():
                        dvs[slot] = dv
                        dks[slot] = dk

                    @pl.when(pair > 0)
                    def _():
                        dvs[slot] += dv
                        dks[slot] += dk
                else:
                    dvs[slot] += dv
                    dks[slot] += dk
                d = dot(kt[slot], score_grad, 1, 0)
                dq_t = d if dq_t is None else dq_t + d
            dq = (dq_t * SCALE).T.astype(LOW)
            dq_ref[row_slot, :, pl.ds(first, width)] = jnp.concatenate(
                [dq[:ROWS], dq[ROWS:]], 1
            )
            return carry

        lax.fori_loop(0, GROUP // 2, step, 0)
    for slot in range(4):
        for j in range(4):
            part = slice(j * ROWS, (j + 1) * ROWS)
            dkv_refs[j][slot, 0] = (dks[slot, part] * SCALE).astype(LOW)
            dkv_refs[j][slot, 1] = dvs[slot, part].astype(LOW)


def attention_grads(place, rows_in, keys_in):
    vmem = pl.BlockSpec(memory_space=pltpu.VMEM)
    width = GROUP * HEAD_SIZE
    kv = jax.ShapeDtypeStruct((4, 2, ROWS, HEAD_SIZE), LOW)
    return pl.pallas_call(
        attention_kernel,
        out_shape=[jax.ShapeDtypeStruct((4, ROWS, width), LOW)] + [kv] * 4,
        in_specs=[pl.BlockSpec(memory_space=pltpu.SMEM)] + [vmem] * 8,
        out_specs=[vmem] * 5,
        scratch_shapes=[
            pltpu.VMEM((4, ROWS, width), LOW),
            pltpu.VMEM((4, ROWS, width), LOW),
            pltpu.VMEM((4, 4 * ROWS, HEAD_SIZE), LOW),
            pltpu.VMEM((4, 4 * ROWS, HEAD_SIZE), LOW),
            pltpu.VMEM((4, HEAD_SIZE, 4 * ROWS), LOW),
            pltpu.VMEM((4, 4 * ROWS, HEAD_SIZE), jnp.float32),
            pltpu.VMEM((4, 4 * ROWS, HEAD_SIZE), jnp.float32),
        ],
        compiler_params=pltpu.CompilerParams(vmem_limit_bytes=48 * 1024 * 1024),
        cost_estimate=pl.CostEstimate(
            flops=20_000_000_000, bytes_accessed=6_000_000, transcendentals=5_000_000
        ),
        name="attention_grads",
    )(place, *rows_in, *keys_in)


def outer_update(outer_grad, params, momentum):
    momentum_out = OUTER_MU * momentum + outer_grad
    params_out = params - OUTER_LR * (outer_grad + OUTER_MU * momentum_out)
    return (params_out, momentum_out)


def swap(value, offset):
    return lax.ppermute(value, "tp", [(i, i ^ offset) for i in range(32)])


def body(queries, keys, values, out_grad, deltas, block_ids, params, momentum):
    index = lax.axis_index("tp")
    y, z = (index // 4) % 4, index % 4
    place = jnp.stack([y, z]).astype(jnp.int32)

    def columns(array, slot, width):
        return lax.dynamic_slice_in_dim(array, (y ^ slot) * width, width, 1)

    with jax.named_scope("keys_values_y"):
        pairs = [
            jnp.stack([columns(keys, k, HEAD_SIZE), columns(values, k, HEAD_SIZE)])
            for k in range(4)
        ]
        by_y = [pairs[0]] + [swap(pairs[k], 4 * k) for k in (1, 2, 3)]
    with jax.named_scope("queries_out_grad_y"):
        width = GROUP * HEAD_SIZE
        rows = [
            jnp.stack([columns(queries, k, width), columns(out_grad, k, width)])
            for k in range(4)
        ]
        rows_in = [rows[0]] + [swap(rows[k], 4 * k) for k in (1, 2, 3)]
    with jax.named_scope("keys_values_z"):
        near = jnp.stack(by_y)
        keys_in = [near] + [swap(near, j) for j in (1, 2, 3)]
    with jax.named_scope("deltas"):
        replicas = lax.axis_size("rep")
        picked = lax.dynamic_slice_in_dim(deltas, block_ids[0] * BLOCK, BLOCK, 0)
        spread = lax.all_to_all(
            picked.reshape(replicas, BLOCK // replicas, -1), "rep", 0, 0, tiled=True
        )
        mean = spread.astype(jnp.float32).sum(0) / replicas
        outer_grad = lax.all_gather(mean, "rep", axis=0, tiled=True)
        params_out, momentum_out = outer_update(outer_grad, params, momentum)
    dq, *dkv = attention_grads(place, rows_in, keys_in)
    with jax.named_scope("query_grad_y"):
        dq_back = [dq[0]] + [swap(dq[k], 4 * k) for k in (1, 2, 3)]
    with jax.named_scope("key_value_grads_z"):
        terms = [dkv[0]] + [swap(dkv[j], j) for j in (1, 2, 3)]
        total = terms[0].astype(jnp.float32)
        for term in terms[1:]:
            total = total + term.astype(jnp.float32)
        total = total.astype(LOW)
    with jax.named_scope("key_value_grads_y"):
        dkv_back = [total[0]] + [swap(total[k], 4 * k) for k in (1, 2, 3)]

    def in_order(slots):
        stacked = jnp.stack(slots)
        return [
            lax.dynamic_index_in_dim(stacked, y ^ g, 0, keepdims=False)
            for g in range(4)
        ]

    query_grad = jnp.concatenate(in_order(dq_back), 1)
    heads = in_order(dkv_back)
    key_gradient = jnp.concatenate([h[0] for h in heads], 1)
    value_gradient = jnp.concatenate([h[1] for h in heads], 1)
    return (query_grad, key_gradient, value_gradient, params_out, momentum_out)


def solution(mesh):
    placed = (
        P(("rep", "tp"), None),
        P(("rep", "tp"), None),
        P(("rep", "tp"), None),
        P(("rep", "tp"), None),
        P("rep", "tp"),
        P(),
        P(None, "tp"),
        P(None, "tp"),
    )
    return jax.shard_map(
        body,
        mesh=mesh,
        in_specs=placed,
        out_specs=(
            P(("rep", "tp"), None),
            P(("rep", "tp"), None),
            P(("rep", "tp"), None),
            P(None, "tp"),
            P(None, "tp"),
        ),
        check_vma=False,
    )
```

```python
import functools
import math

import jax
import jax.numpy as jnp
from jax import lax
from jax.experimental import pallas as pl
from jax.experimental.pallas import tpu as pltpu
from jax.sharding import PartitionSpec as P

QUERY_HEADS = 32
KEY_VALUE_HEADS = 4
HEAD_SIZE = 128
SEQUENCE_LENGTH = 2048
SEQS = 2
BLOCK = 256
ROWS = 128
GROUP = QUERY_HEADS // KEY_VALUE_HEADS
HEADS_AT_ONCE = 4
NEG_FILL = -1e30
OUTER_LR = 0.7
OUTER_MU = 0.9
SCALE = HEAD_SIZE**-0.5
EXP2_SCALE = SCALE * math.log2(math.e)
LOW = jnp.bfloat16


def dot(a, b, dim_a, dim_b):
    return lax.dot_general(
        a, b, (((dim_a,), (dim_b,)), ((), ())), preferred_element_type=jnp.float32
    )


def attention_kernel(place, *refs):
    first_in, second_in, keys_in = refs[:4], refs[4:8], refs[8:12]
    dq_refs, dkv_ref = refs[12:16], refs[16]
    qs, gs, ks, vs, kt, dqs, dks, dvs = refs[17:]
    y, z = place[0], place[1]
    pair, half = 2 * HEAD_SIZE, GROUP * HEAD_SIZE // 2
    for slot in range(4):
        qs[slot, :, :half] = first_in[slot][:, pair:]
        qs[slot, :, half:] = second_in[slot][:, :half]
        gs[slot] = second_in[slot][:, half:]
    for part in range(4):
        for j in range(4):
            at = slice(j * ROWS, (j + 1) * ROWS)
            ks[part, at] = keys_in[j][part ^ y, :, :HEAD_SIZE]
            vs[part, at] = keys_in[j][part ^ y, :, HEAD_SIZE:]
    for part in range(4):
        kt[part] = ks[part].T
    dks[...] = jnp.zeros_like(dks)
    dvs[...] = jnp.zeros_like(dvs)
    width = HEADS_AT_ONCE * HEAD_SIZE
    key_at = lax.broadcasted_iota(jnp.int32, (4 * ROWS, width), 0)
    row_at = lax.broadcasted_iota(jnp.int32, (4 * ROWS, width), 1) & (ROWS - 1)
    key_pos = (((key_at >> 7) ^ z) << 7) + (key_at & (ROWS - 1))
    keep = key_pos <= row_at + (z << 7)

    def down(wide):
        return jnp.concatenate(
            [wide[:, h * HEAD_SIZE : (h + 1) * HEAD_SIZE] for h in range(HEADS_AT_ONCE)], 0
        )

    def step(turn, carry):
        first = pl.multiple_of(turn * width, width)
        for group in range(3, -1, -1):
            row_slot = group ^ y
            q = down(qs[row_slot, :, pl.ds(first, width)])
            g = down(gs[row_slot, :, pl.ds(first, width)])
            scores = []
            peak = None
            for part in range(group + 1):
                s = dot(ks[part], q, 1, 1)
                if part == group:
                    s = jnp.where(keep, s, NEG_FILL)
                scores.append(s)
                top = jnp.max(s, axis=0, keepdims=True)
                peak = top if peak is None else jnp.maximum(peak, top)
            shift = peak * EXP2_SCALE
            weights, prob_grads = [], []
            total = inner = None
            for part in range(group + 1):
                prob_grad = dot(vs[part], g, 1, 1)
                weight = jnp.exp2(scores[part] * EXP2_SCALE - shift)
                total_part = jnp.sum(weight, axis=0, keepdims=True)
                inner_part = jnp.sum(weight * prob_grad, axis=0, keepdims=True)
                total = total_part if total is None else total + total_part
                inner = inner_part if inner is None else inner + inner_part
                weights.append(weight)
                prob_grads.append(prob_grad)
            inverse = 1.0 / total
            inner = inner * inverse
            dq_t = None
            for part in range(group + 1):
                prob = weights[part] * inverse
                prob_low = prob.astype(LOW)
                score_grad = (prob * (prob_grads[part] - inner)).astype(LOW)
                dvs[part] += dot(prob_low, g, 1, 0)
                dks[part] += dot(score_grad, q, 1, 0)
                d = dot(kt[part], score_grad, 1, 0)
                dq_t = d if dq_t is None else dq_t + d
            dq = (dq_t * SCALE).T.astype(LOW)
            for h in range(HEADS_AT_ONCE):
                at = pl.ds(pl.multiple_of(first + h * HEAD_SIZE, HEAD_SIZE), HEAD_SIZE)
                dqs[row_slot, :, at] = dq[h * ROWS : (h + 1) * ROWS]
        return carry

    lax.fori_loop(0, GROUP // HEADS_AT_ONCE, step, 0)
    for slot in range(4):
        dq_refs[slot][...] = dqs[slot]
    for part in range(4):
        for j in range(4):
            at = slice(j * ROWS, (j + 1) * ROWS)
            dkv_ref[z ^ j, part ^ y, 0] = (dks[part, at] * SCALE).astype(LOW)
            dkv_ref[z ^ j, part ^ y, 1] = dvs[part, at].astype(LOW)


def attention_grads(place, first_in, second_in, keys_in):
    vmem = pl.BlockSpec(memory_space=pltpu.VMEM)
    width = GROUP * HEAD_SIZE
    kv = jax.ShapeDtypeStruct((4, 4, 2, ROWS, HEAD_SIZE), LOW)
    return pl.pallas_call(
        attention_kernel,
        out_shape=[jax.ShapeDtypeStruct((ROWS, width), LOW)] * 4 + [kv],
        in_specs=[pl.BlockSpec(memory_space=pltpu.SMEM)] + [vmem] * 12,
        out_specs=[vmem] * 5,
        scratch_shapes=[
            pltpu.VMEM((4, ROWS, width), LOW),
            pltpu.VMEM((4, ROWS, width), LOW),
            pltpu.VMEM((4, 4 * ROWS, HEAD_SIZE), LOW),
            pltpu.VMEM((4, 4 * ROWS, HEAD_SIZE), LOW),
            pltpu.VMEM((4, HEAD_SIZE, 4 * ROWS), LOW),
            pltpu.VMEM((4, ROWS, width), LOW),
            pltpu.VMEM((4, 4 * ROWS, HEAD_SIZE), jnp.float32),
            pltpu.VMEM((4, 4 * ROWS, HEAD_SIZE), jnp.float32),
        ],
        compiler_params=pltpu.CompilerParams(vmem_limit_bytes=20 * 1024 * 1024),
        cost_estimate=pl.CostEstimate(
            flops=20_000_000_000, bytes_accessed=6_000_000, transcendentals=5_000_000
        ),
        name="attention_grads",
    )(place, *first_in, *second_in, *keys_in)


def pack_first_kernel(place, keys, values, queries, *out):
    y = place[0]
    half = GROUP * HEAD_SIZE // 2
    for k in range(4):
        head = pl.ds(pl.multiple_of((y ^ k) * HEAD_SIZE, HEAD_SIZE), HEAD_SIZE)
        out[k][:, :HEAD_SIZE] = keys[:, head]
        out[k][:, HEAD_SIZE : 2 * HEAD_SIZE] = values[:, head]
        rows = pl.ds(pl.multiple_of((y ^ k) * 2 * half, 2 * half), half)
        out[k][:, 2 * HEAD_SIZE :] = queries[:, rows]


def pack_second_kernel(place, queries, out_grad, *out):
    y = place[0]
    half = GROUP * HEAD_SIZE // 2
    for k in range(4):
        first = pl.multiple_of((y ^ k) * 2 * half, half)
        out[k][:, :half] = queries[:, pl.ds(first + half, half)]
        out[k][:, half:] = out_grad[:, pl.ds(first, 2 * half)]


def pack(kernel, name, width, place, *arrays):
    vmem = pl.BlockSpec(memory_space=pltpu.VMEM)
    return pl.pallas_call(
        kernel,
        out_shape=[jax.ShapeDtypeStruct((ROWS, width), LOW)] * 4,
        in_specs=[pl.BlockSpec(memory_space=pltpu.SMEM)] + [vmem] * len(arrays),
        out_specs=[vmem] * 4,
        cost_estimate=pl.CostEstimate(
            flops=0, bytes_accessed=16 * ROWS * width, transcendentals=0
        ),
        name=name,
    )(place, *arrays)


def unpack_pairs_kernel(place, *refs):
    y = place[0]
    for k in range(4):
        head = pl.ds(pl.multiple_of((y ^ k) * HEAD_SIZE, HEAD_SIZE), HEAD_SIZE)
        refs[4][:, head] = refs[k][0]
        refs[5][:, head] = refs[k][1]


def unpack_pairs(place, back):
    vmem = pl.BlockSpec(memory_space=pltpu.VMEM)
    return pl.pallas_call(
        unpack_pairs_kernel,
        out_shape=[jax.ShapeDtypeStruct((ROWS, KEY_VALUE_HEADS * HEAD_SIZE), LOW)] * 2,
        in_specs=[pl.BlockSpec(memory_space=pltpu.SMEM)] + [vmem] * 4,
        out_specs=[vmem] * 2,
        cost_estimate=pl.CostEstimate(flops=0, bytes_accessed=500_000, transcendentals=0),
        name="unpack_pairs",
    )(place, *back)


def outer_update(outer_grad, params, momentum):
    momentum_out = OUTER_MU * momentum + outer_grad
    params_out = params - OUTER_LR * (outer_grad + OUTER_MU * momentum_out)
    return (params_out, momentum_out)


ALONG_Y = [[16 * s + 4 * y + z for y in range(4)] for s in range(2) for z in range(4)]
ALONG_Z = [[16 * s + 4 * y + z for z in range(4)] for s in range(2) for y in range(4)]


def swap(value, offset):
    return lax.ppermute(value, "tp", [(i, i ^ offset) for i in range(32)])


def shift(value, step):
    return lax.ppermute(
        value, "tp", [(i, i // 4 * 4 + (i + step) % 4) for i in range(32)]
    )


def exchange(value, groups):
    return lax.all_to_all(value, "tp", 0, 0, axis_index_groups=groups, tiled=True)


def body(queries, keys, values, out_grad, deltas, block_ids, params, momentum):
    index = lax.axis_index("tp")
    y, z = (index // 4) % 4, index % 4
    place = jnp.stack([y, z]).astype(jnp.int32)
    replicas = lax.axis_size("rep")

    def swapped(parts):
        return [parts[0]] + [swap(parts[k], 4 * k) for k in (1, 2, 3)]

    half = GROUP * HEAD_SIZE // 2
    pair = 2 * HEAD_SIZE
    first = pack(
        pack_first_kernel, "pack_first", pair + half, place, keys, values, queries
    )
    place_then, *first = lax.optimization_barrier((place, *first))
    second = pack(
        pack_second_kernel, "pack_second", 3 * half, place_then, queries, out_grad
    )
    with jax.named_scope("keys_values_y"):
        first_in = swapped(first)
    with jax.named_scope("queries_out_grad_y"):
        second_in = swapped(second)
    with jax.named_scope("keys_values_z"):
        near = jnp.stack([part[:, :pair] for part in first_in])
        keys_in = [near] + [swap(near, j) for j in (1, 2, 3)]
    with jax.named_scope("deltas"):
        picked = lax.dynamic_slice_in_dim(deltas, block_ids[0] * BLOCK, BLOCK, 0)
        spread = lax.all_to_all(
            picked.reshape(replicas, BLOCK // replicas, -1), "rep", 0, 0, tiled=True
        )
        mean = spread.astype(jnp.float32).sum(0) / replicas
        outer_grad = lax.all_to_all(
            jnp.broadcast_to(mean, (replicas,) + mean.shape), "rep", 0, 0, tiled=True
        ).reshape(BLOCK, -1)
        params_out, momentum_out = outer_update(outer_grad, params, momentum)
    *dq, dkv = attention_grads(place, first_in, second_in, keys_in)
    with jax.named_scope("key_value_grads_z"):
        terms = exchange(dkv, ALONG_Z)
    with jax.named_scope("query_grad_y"):
        dq_back = swapped(dq)
    with jax.named_scope("key_value_grads_y"):
        total = terms.astype(jnp.float32).sum(0).astype(LOW)
        dkv_back = swapped(total)
        key_gradient, value_gradient = unpack_pairs(place, dkv_back)
    with jax.named_scope("query_grad"):
        stacked = jnp.stack(dq_back)
        query_grad = jnp.concatenate(
            [
                lax.dynamic_index_in_dim(stacked, y ^ g, 0, keepdims=False)
                for g in range(4)
            ],
            1,
        )
    return (query_grad, key_gradient, value_gradient, params_out, momentum_out)


def solution(mesh):
    placed = (
        P(("rep", "tp"), None),
        P(("rep", "tp"), None),
        P(("rep", "tp"), None),
        P(("rep", "tp"), None),
        P("rep", "tp"),
        P(),
        P(None, "tp"),
        P(None, "tp"),
    )
    return jax.shard_map(
        body,
        mesh=mesh,
        in_specs=placed,
        out_specs=(
            P(("rep", "tp"), None),
            P(("rep", "tp"), None),
            P(("rep", "tp"), None),
            P(None, "tp"),
            P(None, "tp"),
        ),
        check_vma=False,
    )
```

```python
import functools
import math

import jax
import jax.numpy as jnp
from jax import lax
from jax.experimental import pallas as pl
from jax.experimental.pallas import tpu as pltpu
from jax.sharding import PartitionSpec as P

QUERY_HEADS = 32
KEY_VALUE_HEADS = 4
HEAD_SIZE = 128
SEQUENCE_LENGTH = 2048
SEQS = 2
BLOCK = 256
ROWS = 128
GROUP = QUERY_HEADS // KEY_VALUE_HEADS
VMEM_LIMIT = 60 * 1024 * 1024
HEADS_AT_ONCE = 4
NEG_FILL = -1e30
OUTER_LR = 0.7
OUTER_MU = 0.9
SCALE = HEAD_SIZE**-0.5
EXP2_SCALE = SCALE * math.log2(math.e)
LOW = jnp.bfloat16


def place_of():
    index = lax.axis_index("tp")
    return (index >> 2) & 3, index & 3


def dot(a, b, dim_a, dim_b):
    return lax.dot_general(
        a, b, (((dim_a,), (dim_b,)), ((), ())), preferred_element_type=jnp.float32
    )


def copy_all(copies, sems):
    started = [
        pltpu.make_async_copy(source, to, sems.at[n])
        for n, (source, to) in enumerate(copies)
    ]
    for copy in started:
        copy.start()
    for copy in started:
        copy.wait()


def attention_kernel(*refs):
    first_in, second_in, keys_in = refs[:4], refs[4:8], refs[8:12]
    dq_refs, dkv_ref = refs[12:16], refs[16]
    qs, gs, ks, vs, kt, dqs, dks, dvs, dkvs, sems = refs[17:]
    y, z = place_of()
    pair, half = 2 * HEAD_SIZE, GROUP * HEAD_SIZE // 2
    copies = []
    for slot in range(4):
        copies += [
            (first_in[slot].at[:, pair:], qs.at[slot, :, :half]),
            (second_in[slot].at[:, :half], qs.at[slot, :, half:]),
            (second_in[slot].at[:, half:], gs.at[slot]),
        ]
    for part in range(4):
        for j in range(4):
            at = slice(j * ROWS, (j + 1) * ROWS)
            copies += [
                (keys_in[j].at[part ^ y, :, :HEAD_SIZE], ks.at[part, at]),
                (keys_in[j].at[part ^ y, :, HEAD_SIZE:], vs.at[part, at]),
            ]
    copy_all(copies, sems)
    for part in range(4):
        kt[part] = ks[part].T
    dks[...] = jnp.zeros_like(dks)
    dvs[...] = jnp.zeros_like(dvs)
    width = HEADS_AT_ONCE * HEAD_SIZE
    key_at = lax.broadcasted_iota(jnp.int32, (4 * ROWS, width), 0)
    row_at = lax.broadcasted_iota(jnp.int32, (4 * ROWS, width), 1) & (ROWS - 1)
    key_pos = (((key_at >> 7) ^ z) << 7) + (key_at & (ROWS - 1))
    keep = key_pos <= row_at + (z << 7)

    def down(wide):
        return jnp.concatenate(
            [wide[:, h * HEAD_SIZE : (h + 1) * HEAD_SIZE] for h in range(HEADS_AT_ONCE)], 0
        )

    def step(turn, carry):
        first = pl.multiple_of(turn * width, width)
        state = {}

        def find_scores(group):
            q = down(qs[group ^ y, :, pl.ds(first, width)])
            scores = []
            peak = None
            for part in range(group + 1):
                s = dot(ks[part], q, 1, 1)
                if part == group:
                    s = jnp.where(keep, s, NEG_FILL)
                scores.append(s)
                top = jnp.max(s, axis=0, keepdims=True)
                peak = top if peak is None else jnp.maximum(peak, top)
            state[group] = (q, scores, peak * EXP2_SCALE)

        def find_weights(group):
            q, scores, shift = state[group]
            g = down(gs[group ^ y, :, pl.ds(first, width)])
            weights, prob_grads = [], []
            total = inner = None
            for part in range(group + 1):
                prob_grad = dot(vs[part], g, 1, 1)
                weight = jnp.exp2(scores[part] * EXP2_SCALE - shift)
                total_part = jnp.sum(weight, axis=0, keepdims=True)
                inner_part = jnp.sum(weight * prob_grad, axis=0, keepdims=True)
                total = total_part if total is None else total + total_part
                inner = inner_part if inner is None else inner + inner_part
                weights.append(weight)
                prob_grads.append(prob_grad)
            inverse = 1.0 / total
            state[group] = (q, g, weights, prob_grads, inverse, inner * inverse)

        def find_grads(group):
            q, g, weights, prob_grads, inverse, inner = state.pop(group)
            dq_t = None
            for part in range(group + 1):
                prob = weights[part] * inverse
                prob_low = prob.astype(LOW)
                score_grad = (prob * (prob_grads[part] - inner)).astype(LOW)
                dvs[part] += dot(prob_low, g, 1, 0)
                dks[part] += dot(score_grad, q, 1, 0)
                d = dot(kt[part], score_grad, 1, 0)
                dq_t = d if dq_t is None else dq_t + d
            dq = (dq_t * SCALE).T.astype(LOW)
            for h in range(HEADS_AT_ONCE):
                at = pl.ds(pl.multiple_of(first + h * HEAD_SIZE, HEAD_SIZE), HEAD_SIZE)
                dqs[group ^ y, :, at] = dq[h * ROWS : (h + 1) * ROWS]

        find_scores(3)
        find_weights(3)
        for group in (2, 1, 0):
            find_scores(group)
            find_grads(group + 1)
            find_weights(group)
        find_grads(0)
        return carry

    lax.fori_loop(0, GROUP // HEADS_AT_ONCE, step, 0)
    for part in range(4):
        for j in range(4):
            at = slice(j * ROWS, (j + 1) * ROWS)
            dkvs[z ^ j, part ^ y, 0] = (dks[part, at] * SCALE).astype(LOW)
            dkvs[z ^ j, part ^ y, 1] = dvs[part, at].astype(LOW)
    copy_all(
        [(dkvs, dkv_ref)] + [(dqs.at[slot], dq_refs[slot]) for slot in range(4)],
        sems,
    )


def attention_grads(first_in, second_in, keys_in):
    anywhere = pl.BlockSpec(memory_space=pl.ANY)
    width = GROUP * HEAD_SIZE
    kv = jax.ShapeDtypeStruct((4, 4, 2, ROWS, HEAD_SIZE), LOW)
    return pl.pallas_call(
        attention_kernel,
        out_shape=[jax.ShapeDtypeStruct((ROWS, width), LOW)] * 4 + [kv],
        in_specs=[anywhere] * 12,
        out_specs=[anywhere] * 5,
        scratch_shapes=[
            pltpu.VMEM((4, ROWS, width), LOW),
            pltpu.VMEM((4, ROWS, width), LOW),
            pltpu.VMEM((4, 4 * ROWS, HEAD_SIZE), LOW),
            pltpu.VMEM((4, 4 * ROWS, HEAD_SIZE), LOW),
            pltpu.VMEM((4, HEAD_SIZE, 4 * ROWS), LOW),
            pltpu.VMEM((4, ROWS, width), LOW),
            pltpu.VMEM((4, 4 * ROWS, HEAD_SIZE), jnp.float32),
            pltpu.VMEM((4, 4 * ROWS, HEAD_SIZE), jnp.float32),
            pltpu.VMEM((4, 4, 2, ROWS, HEAD_SIZE), LOW),
            pltpu.SemaphoreType.DMA((44,)),
        ],
        compiler_params=pltpu.CompilerParams(vmem_limit_bytes=VMEM_LIMIT),
        cost_estimate=pl.CostEstimate(
            flops=100_000_000_000, bytes_accessed=6_000_000, transcendentals=5_000_000
        ),
        name="attention_grads",
    )(*first_in, *second_in, *keys_in)


def pack_first_kernel(keys, values, queries, *out):
    y, _ = place_of()
    half = GROUP * HEAD_SIZE // 2
    for k in range(4):
        head = pl.ds(pl.multiple_of((y ^ k) * HEAD_SIZE, HEAD_SIZE), HEAD_SIZE)
        out[k][:, :HEAD_SIZE] = keys[:, head]
        out[k][:, HEAD_SIZE : 2 * HEAD_SIZE] = values[:, head]
        rows = pl.ds(pl.multiple_of((y ^ k) * 2 * half, 2 * half), half)
        out[k][:, 2 * HEAD_SIZE :] = queries[:, rows]


def pack_second_kernel(queries, out_grad, *out):
    y, _ = place_of()
    half = GROUP * HEAD_SIZE // 2
    for k in range(4):
        first = pl.multiple_of((y ^ k) * 2 * half, half)
        out[k][:, :half] = queries[:, pl.ds(first + half, half)]
        out[k][:, half:] = out_grad[:, pl.ds(first, 2 * half)]


def pack(kernel, name, width, *arrays):
    vmem = pl.BlockSpec(memory_space=pltpu.VMEM)
    return pl.pallas_call(
        kernel,
        out_shape=[jax.ShapeDtypeStruct((ROWS, width), LOW)] * 4,
        in_specs=[vmem] * len(arrays),
        out_specs=[vmem] * 4,
        cost_estimate=pl.CostEstimate(
            flops=0, bytes_accessed=16 * ROWS * width, transcendentals=0
        ),
        name=name,
    )(*arrays)


def finish_kernel(*refs):
    y, _ = place_of()
    rows, pairs = refs[:4], refs[4:8]
    dq_out, dk_out, dv_out = refs[8:]
    width = GROUP * HEAD_SIZE
    for k in range(4):
        dq_out[:, pl.ds(pl.multiple_of((y ^ k) * width, width), width)] = rows[k][...]
        head = pl.ds(pl.multiple_of((y ^ k) * HEAD_SIZE, HEAD_SIZE), HEAD_SIZE)
        dk_out[:, head] = pairs[k][0]
        dv_out[:, head] = pairs[k][1]


def finish(rows, pairs):
    vmem = pl.BlockSpec(memory_space=pltpu.VMEM)
    heads = jax.ShapeDtypeStruct((ROWS, KEY_VALUE_HEADS * HEAD_SIZE), LOW)
    return pl.pallas_call(
        finish_kernel,
        out_shape=[jax.ShapeDtypeStruct((ROWS, QUERY_HEADS * HEAD_SIZE), LOW), heads, heads],
        in_specs=[vmem] * 8,
        out_specs=[vmem] * 3,
        compiler_params=pltpu.CompilerParams(vmem_limit_bytes=6 * 1024 * 1024),
        cost_estimate=pl.CostEstimate(
            flops=0, bytes_accessed=2_500_000, transcendentals=0
        ),
        name="finish",
    )(*rows, *pairs)


def outer_update(outer_grad, params, momentum):
    momentum_out = OUTER_MU * momentum + outer_grad
    params_out = params - OUTER_LR * (outer_grad + OUTER_MU * momentum_out)
    return (params_out, momentum_out)


ALONG_Y = [[16 * s + 4 * y + z for y in range(4)] for s in range(2) for z in range(4)]
ALONG_Z = [[16 * s + 4 * y + z for z in range(4)] for s in range(2) for y in range(4)]


def swap(value, offset):
    return lax.ppermute(value, "tp", [(i, i ^ offset) for i in range(32)])


def exchange(value, groups):
    return lax.all_to_all(value, "tp", 0, 0, axis_index_groups=groups, tiled=True)


def body(queries, keys, values, out_grad, deltas, block_ids, params, momentum):
    replicas = lax.axis_size("rep")

    def swapped(parts):
        return [parts[0]] + [swap(parts[k], 4 * k) for k in (1, 2, 3)]

    half = GROUP * HEAD_SIZE // 2
    pair = 2 * HEAD_SIZE
    first = pack(
        pack_first_kernel, "pack_first", pair + half, keys, values, queries
    )
    queries, out_grad, *first = lax.optimization_barrier((queries, out_grad, *first))
    second = pack(
        pack_second_kernel, "pack_second", 3 * half, queries, out_grad
    )
    with jax.named_scope("keys_values_y"):
        first_in = swapped(first)
    with jax.named_scope("queries_out_grad_y"):
        second_in = swapped(second)
    with jax.named_scope("keys_values_z"):
        near = jnp.stack([part[:, :pair] for part in first_in])
    with jax.named_scope("deltas"):
        picked = lax.dynamic_slice_in_dim(deltas, block_ids[0] * BLOCK, BLOCK, 0)
        columns = picked.shape[1]
        quarters = picked.reshape(1, 4, 1, BLOCK // 4, columns)
        quarters = jnp.broadcast_to(quarters, (replicas // 8, 4, 2, BLOCK // 4, columns))
        every = lax.all_to_all(
            quarters.reshape(replicas, BLOCK // 4, columns), "rep", 0, 0, tiled=True
        )
    with jax.named_scope("keys_values_z"):
        keys_in = [near] + [swap(near, j) for j in (1, 2, 3)]
    grads = attention_grads(first_in, second_in, keys_in)
    dq, dkv = grads[:4], grads[4]
    dkv, every = lax.optimization_barrier((dkv, every))
    with jax.named_scope("key_value_grads_z"):
        terms = exchange(dkv, ALONG_Z)
    with jax.named_scope("outer_step"):
        outer_grad = every.astype(jnp.float32).sum(0) / replicas
        x = (lax.axis_index("rep") >> 1) & 3
        for bit in (1, 2):
            other = lax.ppermute(
                outer_grad, "rep", [(i, i ^ (2 * bit)) for i in range(replicas)]
            )
            low = jnp.where((x & bit) == 0, outer_grad, other)
            high = jnp.where((x & bit) == 0, other, outer_grad)
            outer_grad = jnp.concatenate([low, high], 0)
        outer_grad, terms = lax.optimization_barrier((outer_grad, terms))
        params_out, momentum_out = outer_update(outer_grad, params, momentum)
    with jax.named_scope("query_grad_y"):
        dq_back = swapped(dq)
    with jax.named_scope("key_value_grads_y"):
        total = terms.astype(jnp.float32).sum(0).astype(LOW)
        dkv_back = swapped(total)
    query_grad, key_gradient, value_gradient = finish(dq_back, dkv_back)
    return (query_grad, key_gradient, value_gradient, params_out, momentum_out)


def solution(mesh):
    placed = (
        P(("rep", "tp"), None),
        P(("rep", "tp"), None),
        P(("rep", "tp"), None),
        P(("rep", "tp"), None),
        P("rep", "tp"),
        P(),
        P(None, "tp"),
        P(None, "tp"),
    )
    return jax.shard_map(
        body,
        mesh=mesh,
        in_specs=placed,
        out_specs=(
            P(("rep", "tp"), None),
            P(("rep", "tp"), None),
            P(("rep", "tp"), None),
            P(None, "tp"),
            P(None, "tp"),
        ),
        check_vma=False,
    )
```

```python
import functools
import math

import jax
import jax.numpy as jnp
from jax import lax
from jax.experimental import pallas as pl
from jax.experimental.pallas import tpu as pltpu
from jax.sharding import PartitionSpec as P

QUERY_HEADS = 32
KEY_VALUE_HEADS = 4
HEAD_SIZE = 128
SEQUENCE_LENGTH = 2048
SEQS = 2
BLOCK = 256
ROWS = 128
GROUP = QUERY_HEADS // KEY_VALUE_HEADS
VMEM_LIMIT = 60 * 1024 * 1024
HEADS_AT_ONCE = 4
NEG_FILL = -1e30
OUTER_LR = 0.7
OUTER_MU = 0.9
SCALE = HEAD_SIZE**-0.5
EXP2_SCALE = SCALE * math.log2(math.e)
LOW = jnp.bfloat16


def place_of():
    index = lax.axis_index("tp")
    return (index >> 2) & 3, index & 3


def dot(a, b, dim_a, dim_b):
    return lax.dot_general(
        a, b, (((dim_a,), (dim_b,)), ((), ())), preferred_element_type=jnp.float32
    )


def start_all(copies, sems):
    started = [
        pltpu.make_async_copy(source, to, sems.at[n])
        for n, (source, to) in enumerate(copies)
    ]
    for copy in started:
        copy.start()
    return started


def attention_kernel(*refs):
    first_in, second_in, keys_in = refs[:4], refs[4:8], refs[8:12]
    dq_refs, dkv_ref = refs[12:16], refs[16]
    qs, gs, ks, vs, kt, dqs, dks, dvs, dkvs, sems = refs[17:]
    y, z = place_of()
    pair, half = 2 * HEAD_SIZE, GROUP * HEAD_SIZE // 2
    copies = []
    for slot in range(4):
        copies += [
            (first_in[slot].at[:, pair:], qs.at[slot, :, :half]),
            (second_in[slot].at[:, :half], qs.at[slot, :, half:]),
            (second_in[slot].at[:, half:], gs.at[slot]),
        ]
    for part in range(4):
        for j in range(4):
            at = slice(j * ROWS, (j + 1) * ROWS)
            copies += [
                (keys_in[j].at[part ^ y, :, :HEAD_SIZE], ks.at[part, at]),
                (keys_in[j].at[part ^ y, :, HEAD_SIZE:], vs.at[part, at]),
            ]
    started = start_all(copies, sems)
    for copy in started[-32:]:
        copy.wait()
    for part in range(4):
        kt[part] = ks[part].T
    dks[...] = jnp.zeros_like(dks)
    dvs[...] = jnp.zeros_like(dvs)
    for copy in started[:-32]:
        copy.wait()
    width = HEADS_AT_ONCE * HEAD_SIZE
    key_at = lax.broadcasted_iota(jnp.int32, (4 * ROWS, width), 0)
    row_at = lax.broadcasted_iota(jnp.int32, (4 * ROWS, width), 1) & (ROWS - 1)
    key_pos = (((key_at >> 7) ^ z) << 7) + (key_at & (ROWS - 1))
    keep = key_pos <= row_at + (z << 7)

    def down(wide):
        return jnp.concatenate(
            [wide[:, h * HEAD_SIZE : (h + 1) * HEAD_SIZE] for h in range(HEADS_AT_ONCE)], 0
        )

    def step(turn, carry):
        first = pl.multiple_of(turn * width, width)
        state = {}

        def find_scores(group):
            q = down(qs[group ^ y, :, pl.ds(first, width)])
            scores = []
            peak = None
            for part in range(group + 1):
                s = dot(ks[part], q, 1, 1)
                if part == group:
                    s = jnp.where(keep, s, NEG_FILL)
                scores.append(s)
                top = jnp.max(s, axis=0, keepdims=True)
                peak = top if peak is None else jnp.maximum(peak, top)
            state[group] = (q, scores, peak * EXP2_SCALE)

        def find_weights(group):
            q, scores, shift = state[group]
            g = down(gs[group ^ y, :, pl.ds(first, width)])
            weights, prob_grads = [], []
            total = inner = None
            for part in range(group + 1):
                prob_grad = dot(vs[part], g, 1, 1)
                weight = jnp.exp2(scores[part] * EXP2_SCALE - shift)
                total_part = jnp.sum(weight, axis=0, keepdims=True)
                inner_part = jnp.sum(weight * prob_grad, axis=0, keepdims=True)
                total = total_part if total is None else total + total_part
                inner = inner_part if inner is None else inner + inner_part
                weights.append(weight)
                prob_grads.append(prob_grad)
            inverse = 1.0 / total
            state[group] = (q, g, weights, prob_grads, inverse, inner * inverse)

        def find_grads(group):
            q, g, weights, prob_grads, inverse, inner = state.pop(group)
            dq_t = None
            for part in range(group + 1):
                prob = weights[part] * inverse
                prob_low = prob.astype(LOW)
                score_grad = (prob * (prob_grads[part] - inner)).astype(LOW)
                dvs[part] += dot(prob_low, g, 1, 0)
                dks[part] += dot(score_grad, q, 1, 0)
                d = dot(kt[part], score_grad, 1, 0)
                dq_t = d if dq_t is None else dq_t + d
            dq = (dq_t * SCALE).T.astype(LOW)
            for h in range(HEADS_AT_ONCE):
                at = pl.ds(pl.multiple_of(first + h * HEAD_SIZE, HEAD_SIZE), HEAD_SIZE)
                dqs[group ^ y, :, at] = dq[h * ROWS : (h + 1) * ROWS]

        find_scores(3)
        find_weights(3)
        for group in (2, 1, 0):
            find_scores(group)
            find_grads(group + 1)
            find_weights(group)
        find_grads(0)
        return carry

    lax.fori_loop(0, GROUP // HEADS_AT_ONCE, step, 0)
    started = start_all([(dqs.at[slot], dq_refs[slot]) for slot in range(4)], sems)
    for part in range(4):
        for j in range(4):
            at = slice(j * ROWS, (j + 1) * ROWS)
            dkvs[z ^ j, part ^ y, 0] = (dks[part, at] * SCALE).astype(LOW)
            dkvs[z ^ j, part ^ y, 1] = dvs[part, at].astype(LOW)
    last = pltpu.make_async_copy(dkvs, dkv_ref, sems.at[4])
    last.start()
    for copy in started:
        copy.wait()
    last.wait()


def attention_grads(first_in, second_in, keys_in):
    anywhere = pl.BlockSpec(memory_space=pl.ANY)
    width = GROUP * HEAD_SIZE
    kv = jax.ShapeDtypeStruct((4, 4, 2, ROWS, HEAD_SIZE), LOW)
    return pl.pallas_call(
        attention_kernel,
        out_shape=[jax.ShapeDtypeStruct((ROWS, width), LOW)] * 4 + [kv],
        in_specs=[anywhere] * 12,
        out_specs=[anywhere] * 5,
        scratch_shapes=[
            pltpu.VMEM((4, ROWS, width), LOW),
            pltpu.VMEM((4, ROWS, width), LOW),
            pltpu.VMEM((4, 4 * ROWS, HEAD_SIZE), LOW),
            pltpu.VMEM((4, 4 * ROWS, HEAD_SIZE), LOW),
            pltpu.VMEM((4, HEAD_SIZE, 4 * ROWS), LOW),
            pltpu.VMEM((4, ROWS, width), LOW),
            pltpu.VMEM((4, 4 * ROWS, HEAD_SIZE), jnp.float32),
            pltpu.VMEM((4, 4 * ROWS, HEAD_SIZE), jnp.float32),
            pltpu.VMEM((4, 4, 2, ROWS, HEAD_SIZE), LOW),
            pltpu.SemaphoreType.DMA((44,)),
        ],
        compiler_params=pltpu.CompilerParams(vmem_limit_bytes=VMEM_LIMIT),
        cost_estimate=pl.CostEstimate(
            flops=100_000_000_000, bytes_accessed=6_000_000, transcendentals=5_000_000
        ),
        name="attention_grads",
    )(*first_in, *second_in, *keys_in)


def pack_first_kernel(keys, values, queries, *out):
    y, _ = place_of()
    half = GROUP * HEAD_SIZE // 2
    for k in range(4):
        head = pl.ds(pl.multiple_of((y ^ k) * HEAD_SIZE, HEAD_SIZE), HEAD_SIZE)
        out[k][:, :HEAD_SIZE] = keys[:, head]
        out[k][:, HEAD_SIZE : 2 * HEAD_SIZE] = values[:, head]
        rows = pl.ds(pl.multiple_of((y ^ k) * 2 * half, 2 * half), half)
        out[k][:, 2 * HEAD_SIZE :] = queries[:, rows]


def pack_second_kernel(queries, out_grad, *out):
    y, _ = place_of()
    half = GROUP * HEAD_SIZE // 2
    for k in range(4):
        first = pl.multiple_of((y ^ k) * 2 * half, half)
        out[k][:, :half] = queries[:, pl.ds(first + half, half)]
        out[k][:, half:] = out_grad[:, pl.ds(first, 2 * half)]


def pack(kernel, name, width, *arrays):
    vmem = pl.BlockSpec(memory_space=pltpu.VMEM)
    return pl.pallas_call(
        kernel,
        out_shape=[jax.ShapeDtypeStruct((ROWS, width), LOW)] * 4,
        in_specs=[vmem] * len(arrays),
        out_specs=[vmem] * 4,
        cost_estimate=pl.CostEstimate(
            flops=0, bytes_accessed=16 * ROWS * width, transcendentals=0
        ),
        name=name,
    )(*arrays)


def total_kernel(terms, *out):
    for k in range(4):
        total = terms[0, k].astype(jnp.float32)
        for z in range(1, 4):
            total = total + terms[z, k].astype(jnp.float32)
        out[k][...] = total.astype(LOW)


def total_of(terms):
    vmem = pl.BlockSpec(memory_space=pltpu.VMEM)
    return pl.pallas_call(
        total_kernel,
        out_shape=[jax.ShapeDtypeStruct(terms.shape[2:], LOW)] * 4,
        in_specs=[vmem],
        out_specs=[vmem] * 4,
        compiler_params=pltpu.CompilerParams(vmem_limit_bytes=6 * 1024 * 1024),
        cost_estimate=pl.CostEstimate(
            flops=1_000_000, bytes_accessed=1_300_000, transcendentals=0
        ),
        name="total",
    )(terms)


def finish_kernel(*refs):
    y, _ = place_of()
    rows, pairs = refs[:4], refs[4:8]
    dq_out, dk_out, dv_out = refs[8:]
    width = GROUP * HEAD_SIZE
    for k in range(4):
        dq_out[:, pl.ds(pl.multiple_of((y ^ k) * width, width), width)] = rows[k][...]
        head = pl.ds(pl.multiple_of((y ^ k) * HEAD_SIZE, HEAD_SIZE), HEAD_SIZE)
        dk_out[:, head] = pairs[k][0]
        dv_out[:, head] = pairs[k][1]


def finish(rows, pairs):
    vmem = pl.BlockSpec(memory_space=pltpu.VMEM)
    heads = jax.ShapeDtypeStruct((ROWS, KEY_VALUE_HEADS * HEAD_SIZE), LOW)
    return pl.pallas_call(
        finish_kernel,
        out_shape=[jax.ShapeDtypeStruct((ROWS, QUERY_HEADS * HEAD_SIZE), LOW), heads, heads],
        in_specs=[vmem] * 8,
        out_specs=[vmem] * 3,
        compiler_params=pltpu.CompilerParams(vmem_limit_bytes=6 * 1024 * 1024),
        cost_estimate=pl.CostEstimate(
            flops=0, bytes_accessed=2_500_000, transcendentals=0
        ),
        name="finish",
    )(*rows, *pairs)


def outer_update(outer_grad, params, momentum):
    momentum_out = OUTER_MU * momentum + outer_grad
    params_out = params - OUTER_LR * (outer_grad + OUTER_MU * momentum_out)
    return (params_out, momentum_out)


ALONG_Y = [[16 * s + 4 * y + z for y in range(4)] for s in range(2) for z in range(4)]
ALONG_Z = [[16 * s + 4 * y + z for z in range(4)] for s in range(2) for y in range(4)]


def swap(value, offset):
    return lax.ppermute(value, "tp", [(i, i ^ offset) for i in range(32)])


def exchange(value, groups):
    return lax.all_to_all(value, "tp", 0, 0, axis_index_groups=groups, tiled=True)


def body(queries, keys, values, out_grad, deltas, block_ids, params, momentum):
    replicas = lax.axis_size("rep")

    def swapped(parts):
        return [parts[0]] + [swap(parts[k], 4 * k) for k in (1, 2, 3)]

    half = GROUP * HEAD_SIZE // 2
    pair = 2 * HEAD_SIZE
    first = pack(
        pack_first_kernel, "pack_first", pair + half, keys, values, queries
    )
    queries, out_grad, *first = lax.optimization_barrier((queries, out_grad, *first))
    second = pack(
        pack_second_kernel, "pack_second", 3 * half, queries, out_grad
    )
    with jax.named_scope("keys_values_y"):
        first_in = swapped(first)
    with jax.named_scope("queries_out_grad_y"):
        second_in = swapped(second)
    with jax.named_scope("keys_values_z"):
        near = jnp.stack([part[:, :pair] for part in first_in])
    with jax.named_scope("deltas"):
        picked = lax.dynamic_slice_in_dim(deltas, block_ids[0] * BLOCK, BLOCK, 0)
        columns = picked.shape[1]
        halves = picked.reshape(1, 2, 1, BLOCK // 2, columns)
        halves = jnp.broadcast_to(halves, (replicas // 4, 2, 2, BLOCK // 2, columns))
        every = lax.all_to_all(
            halves.reshape(replicas, BLOCK // 2, columns), "rep", 0, 0, tiled=True
        )
    with jax.named_scope("keys_values_z"):
        keys_in = [near] + [swap(near, j) for j in (1, 2, 3)]
    grads = attention_grads(first_in, second_in, keys_in)
    dq, dkv = grads[:4], grads[4]
    dkv, every = lax.optimization_barrier((dkv, every))
    with jax.named_scope("key_value_grads_z"):
        terms = exchange(dkv, ALONG_Z)
    with jax.named_scope("query_grad_y"):
        dq_back = swapped(dq)
    with jax.named_scope("outer_step"):
        outer_grad = every.astype(jnp.float32).sum(0) / replicas
        x = (lax.axis_index("rep") >> 1) & 3
        for bit in (1,):
            other = lax.ppermute(
                outer_grad, "rep", [(i, i ^ (2 * bit)) for i in range(replicas)]
            )
            low = jnp.where((x & bit) == 0, outer_grad, other)
            high = jnp.where((x & bit) == 0, other, outer_grad)
            outer_grad = jnp.concatenate([low, high], 0)
        outer_grad, terms = lax.optimization_barrier((outer_grad, terms))
        params_out, momentum_out = outer_update(outer_grad, params, momentum)
    with jax.named_scope("key_value_grads_y"):
        dkv_back = swapped(total_of(terms))
    query_grad, key_gradient, value_gradient = finish(dq_back, dkv_back)
    return (query_grad, key_gradient, value_gradient, params_out, momentum_out)


def solution(mesh):
    placed = (
        P(("rep", "tp"), None),
        P(("rep", "tp"), None),
        P(("rep", "tp"), None),
        P(("rep", "tp"), None),
        P("rep", "tp"),
        P(),
        P(None, "tp"),
        P(None, "tp"),
    )
    return jax.shard_map(
        body,
        mesh=mesh,
        in_specs=placed,
        out_specs=(
            P(("rep", "tp"), None),
            P(("rep", "tp"), None),
            P(("rep", "tp"), None),
            P(None, "tp"),
            P(None, "tp"),
        ),
        check_vma=False,
    )
```

```python
import functools
import math

import jax
import jax.numpy as jnp
from jax import lax
from jax.experimental import pallas as pl
from jax.experimental.pallas import tpu as pltpu
from jax.sharding import PartitionSpec as P

QUERY_HEADS = 32
KEY_VALUE_HEADS = 4
HEAD_SIZE = 128
SEQUENCE_LENGTH = 2048
SEQS = 2
BLOCK = 256
ROWS = 128
GROUP = QUERY_HEADS // KEY_VALUE_HEADS
VMEM_LIMIT = 60 * 1024 * 1024
HEADS_AT_ONCE = 8
NEG_FILL = -1e30
OUTER_LR = 0.7
OUTER_MU = 0.9
SCALE = HEAD_SIZE**-0.5
EXP2_SCALE = SCALE * math.log2(math.e)
LOW = jnp.bfloat16


def place_of():
    index = lax.axis_index("tp")
    return (index >> 2) & 3, index & 3


def dot(a, b, dim_a, dim_b):
    return lax.dot_general(
        a, b, (((dim_a,), (dim_b,)), ((), ())), preferred_element_type=jnp.float32
    )


def start_all(copies, sems):
    started = [
        pltpu.make_async_copy(source, to, sems.at[n])
        for n, (source, to) in enumerate(copies)
    ]
    for copy in started:
        copy.start()
    return started


def attention_kernel(*refs):
    first_in, second_in, keys_in = refs[:4], refs[4:8], refs[8:12]
    dq_refs, dkv_ref = refs[12:16], refs[16]
    qs, gs, ks, vs, kt, dqs, dks, dvs, dkvs, sems = refs[17:]
    y, z = place_of()
    pair, half = 2 * HEAD_SIZE, GROUP * HEAD_SIZE // 2
    copies = []
    for slot in range(4):
        copies += [
            (first_in[slot].at[:, pair:], qs.at[slot, :, :half]),
            (second_in[slot].at[:, :half], qs.at[slot, :, half:]),
            (second_in[slot].at[:, half:], gs.at[slot]),
        ]
    for part in range(4):
        for j in range(4):
            at = slice(j * ROWS, (j + 1) * ROWS)
            copies += [
                (keys_in[j].at[part ^ y, :, :HEAD_SIZE], ks.at[part, at]),
                (keys_in[j].at[part ^ y, :, HEAD_SIZE:], vs.at[part, at]),
            ]
    started = start_all(copies, sems)
    for copy in started[-32:]:
        copy.wait()
    for part in range(4):
        kt[part] = ks[part].T
    dks[...] = jnp.zeros_like(dks)
    dvs[...] = jnp.zeros_like(dvs)
    for copy in started[:-32]:
        copy.wait()
    width = HEADS_AT_ONCE * HEAD_SIZE
    key_at = lax.broadcasted_iota(jnp.int32, (4 * ROWS, width), 0)
    row_at = lax.broadcasted_iota(jnp.int32, (4 * ROWS, width), 1) & (ROWS - 1)
    key_pos = (((key_at >> 7) ^ z) << 7) + (key_at & (ROWS - 1))
    keep = key_pos <= row_at + (z << 7)

    def down(wide):
        return jnp.concatenate(
            [wide[:, h * HEAD_SIZE : (h + 1) * HEAD_SIZE] for h in range(HEADS_AT_ONCE)], 0
        )

    def step(turn, carry):
        first = pl.multiple_of(turn * width, width)
        state = {}

        def find_scores(group):
            q = down(qs[group ^ y, :, pl.ds(first, width)])
            scores = []
            peak = None
            for part in range(group + 1):
                s = dot(ks[part], q, 1, 1)
                if part == group:
                    s = jnp.where(keep, s, NEG_FILL)
                scores.append(s)
                top = jnp.max(s, axis=0, keepdims=True)
                peak = top if peak is None else jnp.maximum(peak, top)
            state[group] = (q, scores, peak * EXP2_SCALE)

        def find_weights(group):
            q, scores, shift = state[group]
            g = down(gs[group ^ y, :, pl.ds(first, width)])
            weights, prob_grads = [], []
            total = inner = None
            for part in range(group + 1):
                prob_grad = dot(vs[part], g, 1, 1)
                weight = jnp.exp2(scores[part] * EXP2_SCALE - shift)
                total_part = jnp.sum(weight, axis=0, keepdims=True)
                inner_part = jnp.sum(weight * prob_grad, axis=0, keepdims=True)
                total = total_part if total is None else total + total_part
                inner = inner_part if inner is None else inner + inner_part
                weights.append(weight)
                prob_grads.append(prob_grad)
            inverse = 1.0 / total
            state[group] = (q, g, weights, prob_grads, inverse, inner * inverse)

        def find_grads(group):
            q, g, weights, prob_grads, inverse, inner = state.pop(group)
            dq_t = None
            for part in range(group + 1):
                prob = weights[part] * inverse
                prob_low = prob.astype(LOW)
                score_grad = (prob * (prob_grads[part] - inner)).astype(LOW)
                dvs[part] += dot(prob_low, g, 1, 0)
                dks[part] += dot(score_grad, q, 1, 0)
                d = dot(kt[part], score_grad, 1, 0)
                dq_t = d if dq_t is None else dq_t + d
            dq = (dq_t * SCALE).T.astype(LOW)
            for h in range(HEADS_AT_ONCE):
                at = pl.ds(pl.multiple_of(first + h * HEAD_SIZE, HEAD_SIZE), HEAD_SIZE)
                dqs[group ^ y, :, at] = dq[h * ROWS : (h + 1) * ROWS]

        find_scores(3)
        find_weights(3)
        for group in (2, 1, 0):
            find_scores(group)
            find_grads(group + 1)
            find_weights(group)
        find_grads(0)
        return carry

    lax.fori_loop(0, GROUP // HEADS_AT_ONCE, step, 0)
    started = start_all([(dqs.at[slot], dq_refs[slot]) for slot in range(4)], sems)
    for part in range(4):
        for j in range(4):
            at = slice(j * ROWS, (j + 1) * ROWS)
            dkvs[z ^ j, part ^ y, 0] = (dks[part, at] * SCALE).astype(LOW)
            dkvs[z ^ j, part ^ y, 1] = dvs[part, at].astype(LOW)
    last = pltpu.make_async_copy(dkvs, dkv_ref, sems.at[4])
    last.start()
    for copy in started:
        copy.wait()
    last.wait()


def attention_grads(first_in, second_in, keys_in):
    anywhere = pl.BlockSpec(memory_space=pl.ANY)
    width = GROUP * HEAD_SIZE
    kv = jax.ShapeDtypeStruct((4, 4, 2, ROWS, HEAD_SIZE), LOW)
    return pl.pallas_call(
        attention_kernel,
        out_shape=[jax.ShapeDtypeStruct((ROWS, width), LOW)] * 4 + [kv],
        in_specs=[anywhere] * 12,
        out_specs=[anywhere] * 5,
        scratch_shapes=[
            pltpu.VMEM((4, ROWS, width), LOW),
            pltpu.VMEM((4, ROWS, width), LOW),
            pltpu.VMEM((4, 4 * ROWS, HEAD_SIZE), LOW),
            pltpu.VMEM((4, 4 * ROWS, HEAD_SIZE), LOW),
            pltpu.VMEM((4, HEAD_SIZE, 4 * ROWS), LOW),
            pltpu.VMEM((4, ROWS, width), LOW),
            pltpu.VMEM((4, 4 * ROWS, HEAD_SIZE), jnp.float32),
            pltpu.VMEM((4, 4 * ROWS, HEAD_SIZE), jnp.float32),
            pltpu.VMEM((4, 4, 2, ROWS, HEAD_SIZE), LOW),
            pltpu.SemaphoreType.DMA((44,)),
        ],
        compiler_params=pltpu.CompilerParams(vmem_limit_bytes=VMEM_LIMIT),
        cost_estimate=pl.CostEstimate(
            flops=100_000_000_000, bytes_accessed=6_000_000, transcendentals=5_000_000
        ),
        name="attention_grads",
    )(*first_in, *second_in, *keys_in)


def pack_first_kernel(keys, values, queries, *out):
    y, _ = place_of()
    half = GROUP * HEAD_SIZE // 2
    for k in range(4):
        head = pl.ds(pl.multiple_of((y ^ k) * HEAD_SIZE, HEAD_SIZE), HEAD_SIZE)
        out[k][:, :HEAD_SIZE] = keys[:, head]
        out[k][:, HEAD_SIZE : 2 * HEAD_SIZE] = values[:, head]
        rows = pl.ds(pl.multiple_of((y ^ k) * 2 * half, 2 * half), half)
        out[k][:, 2 * HEAD_SIZE :] = queries[:, rows]


def pack_second_kernel(queries, out_grad, *out):
    y, _ = place_of()
    half = GROUP * HEAD_SIZE // 2
    for k in range(4):
        first = pl.multiple_of((y ^ k) * 2 * half, half)
        out[k][:, :half] = queries[:, pl.ds(first + half, half)]
        out[k][:, half:] = out_grad[:, pl.ds(first, 2 * half)]


def pack(kernel, name, width, *arrays):
    vmem = pl.BlockSpec(memory_space=pltpu.VMEM)
    return pl.pallas_call(
        kernel,
        out_shape=[jax.ShapeDtypeStruct((ROWS, width), LOW)] * 4,
        in_specs=[vmem] * len(arrays),
        out_specs=[vmem] * 4,
        cost_estimate=pl.CostEstimate(
            flops=0, bytes_accessed=16 * ROWS * width, transcendentals=0
        ),
        name=name,
    )(*arrays)


def total_kernel(terms, *out):
    for k in range(4):
        total = terms[0, k].astype(jnp.float32)
        for z in range(1, 4):
            total = total + terms[z, k].astype(jnp.float32)
        out[k][...] = total.astype(LOW)


def total_of(terms):
    vmem = pl.BlockSpec(memory_space=pltpu.VMEM)
    return pl.pallas_call(
        total_kernel,
        out_shape=[jax.ShapeDtypeStruct(terms.shape[2:], LOW)] * 4,
        in_specs=[vmem],
        out_specs=[vmem] * 4,
        compiler_params=pltpu.CompilerParams(vmem_limit_bytes=6 * 1024 * 1024),
        cost_estimate=pl.CostEstimate(
            flops=1_000_000, bytes_accessed=1_300_000, transcendentals=0
        ),
        name="total",
    )(terms)


def finish_kernel(*refs):
    y, _ = place_of()
    rows, pairs = refs[:4], refs[4:8]
    dq_out, dk_out, dv_out = refs[8:]
    width = GROUP * HEAD_SIZE
    for k in range(4):
        dq_out[:, pl.ds(pl.multiple_of((y ^ k) * width, width), width)] = rows[k][...]
        head = pl.ds(pl.multiple_of((y ^ k) * HEAD_SIZE, HEAD_SIZE), HEAD_SIZE)
        dk_out[:, head] = pairs[k][0]
        dv_out[:, head] = pairs[k][1]


def finish(rows, pairs):
    vmem = pl.BlockSpec(memory_space=pltpu.VMEM)
    heads = jax.ShapeDtypeStruct((ROWS, KEY_VALUE_HEADS * HEAD_SIZE), LOW)
    return pl.pallas_call(
        finish_kernel,
        out_shape=[jax.ShapeDtypeStruct((ROWS, QUERY_HEADS * HEAD_SIZE), LOW), heads, heads],
        in_specs=[vmem] * 8,
        out_specs=[vmem] * 3,
        compiler_params=pltpu.CompilerParams(vmem_limit_bytes=6 * 1024 * 1024),
        cost_estimate=pl.CostEstimate(
            flops=0, bytes_accessed=2_500_000, transcendentals=0
        ),
        name="finish",
    )(*rows, *pairs)


def outer_update(outer_grad, params, momentum):
    momentum_out = OUTER_MU * momentum + outer_grad
    params_out = params - OUTER_LR * (outer_grad + OUTER_MU * momentum_out)
    return (params_out, momentum_out)


ALONG_Y = [[16 * s + 4 * y + z for y in range(4)] for s in range(2) for z in range(4)]
ALONG_Z = [[16 * s + 4 * y + z for z in range(4)] for s in range(2) for y in range(4)]


def swap(value, offset):
    return lax.ppermute(value, "tp", [(i, i ^ offset) for i in range(32)])


def exchange(value, groups):
    return lax.all_to_all(value, "tp", 0, 0, axis_index_groups=groups, tiled=True)


def body(queries, keys, values, out_grad, deltas, block_ids, params, momentum):
    replicas = lax.axis_size("rep")

    def swapped(parts):
        return [parts[0]] + [swap(parts[k], 4 * k) for k in (1, 2, 3)]

    half = GROUP * HEAD_SIZE // 2
    pair = 2 * HEAD_SIZE
    first = pack(
        pack_first_kernel, "pack_first", pair + half, keys, values, queries
    )
    queries, out_grad, *first = lax.optimization_barrier((queries, out_grad, *first))
    second = pack(
        pack_second_kernel, "pack_second", 3 * half, queries, out_grad
    )
    with jax.named_scope("keys_values_y"):
        first_in = swapped(first)
    with jax.named_scope("queries_out_grad_y"):
        second_in = swapped(second)
    with jax.named_scope("keys_values_z"):
        near = jnp.stack([part[:, :pair] for part in first_in])
    with jax.named_scope("deltas"):
        picked = lax.dynamic_slice_in_dim(deltas, block_ids[0] * BLOCK, BLOCK, 0)
        columns = picked.shape[1]
        halves = picked.reshape(1, 2, 1, BLOCK // 2, columns)
        halves = jnp.broadcast_to(halves, (replicas // 4, 2, 2, BLOCK // 2, columns))
        every = lax.all_to_all(
            halves.reshape(replicas, BLOCK // 2, columns), "rep", 0, 0, tiled=True
        )
    with jax.named_scope("keys_values_z"):
        keys_in = [near] + [swap(near, j) for j in (1, 2, 3)]
    grads = attention_grads(first_in, second_in, keys_in)
    dq, dkv = grads[:4], grads[4]
    dkv, every = lax.optimization_barrier((dkv, every))
    with jax.named_scope("key_value_grads_z"):
        terms = exchange(dkv, ALONG_Z)
    with jax.named_scope("query_grad_y"):
        dq_back = swapped(dq)
    with jax.named_scope("outer_step"):
        outer_grad = every.astype(jnp.float32).sum(0) / replicas
        x = (lax.axis_index("rep") >> 1) & 3
        for bit in (1,):
            other = lax.ppermute(
                outer_grad, "rep", [(i, i ^ (2 * bit)) for i in range(replicas)]
            )
            low = jnp.where((x & bit) == 0, outer_grad, other)
            high = jnp.where((x & bit) == 0, other, outer_grad)
            outer_grad = jnp.concatenate([low, high], 0)
        outer_grad, terms = lax.optimization_barrier((outer_grad, terms))
        params_out, momentum_out = outer_update(outer_grad, params, momentum)
    with jax.named_scope("key_value_grads_y"):
        dkv_back = swapped(total_of(terms))
    query_grad, key_gradient, value_gradient = finish(dq_back, dkv_back)
    return (query_grad, key_gradient, value_gradient, params_out, momentum_out)


def solution(mesh):
    placed = (
        P(("rep", "tp"), None),
        P(("rep", "tp"), None),
        P(("rep", "tp"), None),
        P(("rep", "tp"), None),
        P("rep", "tp"),
        P(),
        P(None, "tp"),
        P(None, "tp"),
    )
    return jax.shard_map(
        body,
        mesh=mesh,
        in_specs=placed,
        out_specs=(
            P(("rep", "tp"), None),
            P(("rep", "tp"), None),
            P(("rep", "tp"), None),
            P(None, "tp"),
            P(None, "tp"),
        ),
        check_vma=False,
    )
```
